32 devices in a mesh: rows: 8 (over z, x), grp: 4 (over y, core).
Axes of the slice: x: 2, y: 2, z: 4, core: 2. Of those that a mesh axis runs over, the one named last changes fastest.
Arguments:
- embeddings: bfloat16 [16384, 1024], P(('rows', 'grp')), may hold values from -6 to 6
- coarse_ids: int32 [16384], P(('rows', 'grp')), may hold values from 0 to 2047, as said below
- fine_ids: int32 [16384], P(('rows', 'grp')), may hold values from 0 to 63, as said below
- coarse_old: float32 [2048, 1024], P(('rows', 'grp')), may hold values from -6 to 6
- fine_old: float32 [2048, 64, 1024], P('rows', 'grp'), may hold values from -6 to 6
Outputs:
- coarse_new: float32 [2048, 1024], P(('rows', 'grp'))
- fine_new: float32 [2048, 64, 1024], P('rows', 'grp')
- distances: float32 [16384], P(('rows', 'grp'))
The draws below stay inside these ranges and needn't reach their ends.
Inputs may be any that keep to these rules, and one draw needn't show every extreme that they name: Among the 512 rows of one device, at most 32 have the same pair (coarse_ids // 256, fine_ids // 16), and in every such block some pair has exactly 32. `fine_ids`: within each coarse cluster's fine centroids.
All inputs are finite; a program needn't handle non-finite values.
Results may differ from the reference program's by a relative error of at most 0.0003.
Values may be sent and summed in bfloat16 or wider, within the bound.
A program may use at most 128 MiB of HBM per device.

```python
import jax
import jax.numpy as jnp

D = 1024
K = 2048
F = 64
ROWS_DEV = 512
SLOTS = 32
KC = 256
FG = 16
TOTAL_ROWS = 16384
N_GRP = 4
DEVICES = 32


def route_ids(key):
    dests = DEVICES
    total_slots = dests * SLOTS

    def one_block(block_key):
        parts = jax.random.split(block_key, 6)
        hotness = (jax.random.randint(parts[0], (dests,), 0, 4) == 0).astype(jnp.int32)
        first_dest = jax.random.randint(parts[1], (), 0, dests)
        slot_index = jnp.arange(total_slots, dtype=jnp.int32)
        owner_of = slot_index // SLOTS
        priority = jax.random.randint(parts[2], (total_slots,), 0, 2 ** 15)
        priority = priority - hotness[owner_of] * 2 ** 14 - (owner_of == first_dest).astype(jnp.int32) * 2 ** 16
        scores = priority * 8192 + slot_index
        chosen = jnp.argsort(scores, stable=True)[:ROWS_DEV]
        chosen = jax.random.permutation(parts[3], chosen)
        target = chosen // SLOTS
        coarse = target // N_GRP * KC + jax.random.randint(parts[4], (ROWS_DEV,), 0, KC)
        fine = target % N_GRP * FG + jax.random.randint(parts[5], (ROWS_DEV,), 0, FG)
        return (coarse.astype(jnp.int32), fine.astype(jnp.int32))
    block_keys = jax.random.split(jax.random.fold_in(key, 7), DEVICES)
    coarse, fine = jax.vmap(one_block)(block_keys)
    return (coarse.reshape(-1), fine.reshape(-1))


def draw_coarse_ids(key, part):
    return route_ids(key)[0]


def draw_fine_ids(key, part):
    return route_ids(key)[1]


def block_scale(stream_key, extent, cuts, smallest, high):
    gain, own = 1.0, jax.random.fold_in(stream_key, 6)
    for axis_at, blocks in cuts:
        steps = jnp.exp(jax.random.uniform(jax.random.fold_in(own, axis_at), (blocks,), jnp.float32, smallest / len(cuts), high / len(cuts)))
        gain = gain * jnp.repeat(steps, extent[axis_at] // blocks).reshape([-1 if axis == axis_at else 1 for axis in range(len(extent))])
    return gain


def normal_values(own_key, shape, scale, reach, cuts=(), kind=jnp.bfloat16):
    factor_of = block_scale(own_key, shape, cuts, -0.22, 0.18) if cuts else 1.0
    result = jax.random.normal(own_key, shape, jnp.float32) * scale * factor_of
    return jnp.minimum(jnp.maximum(result, -reach), reach).astype(kind)


def setup_inputs(seed: int = 0) -> dict:
    seeds = jax.random.split(jax.random.key(seed), 6)
    return {
        "embeddings": normal_values(seeds[0], (TOTAL_ROWS, D), 1.0, 6.0, ((0, 32),)),
        "coarse_ids": draw_coarse_ids(jax.random.fold_in(seeds[5], 71), 0),
        "fine_ids": draw_fine_ids(jax.random.fold_in(seeds[5], 71), 0),
        "coarse_old": normal_values(seeds[3], (K, D), 1.0, 6.0, ((0, 32),), jnp.float32),
        "fine_old": normal_values(seeds[4], (K, F, D), 1.0, 6.0, ((0, 8), (1, 4)), jnp.float32),
    }


def reference(embeddings, coarse_ids, fine_ids, coarse_old, fine_old):
    values = embeddings.astype(jnp.float32)
    ones_rows = jnp.ones((embeddings.shape[0],), jnp.float32)
    fine_index = coarse_ids * F + fine_ids
    fine_sums = jax.ops.segment_sum(values, fine_index, num_segments=K * F)
    fine_counts = jax.ops.segment_sum(ones_rows, fine_index, num_segments=K * F)
    fine_flat = (fine_old.reshape(K * F, D) + fine_sums) / (1.0 + fine_counts)[:, None]
    coarse_sums = jax.ops.segment_sum(values, coarse_ids, num_segments=K)
    coarse_counts = jax.ops.segment_sum(ones_rows, coarse_ids, num_segments=K)
    coarse_new = (coarse_old + coarse_sums) / (1.0 + coarse_counts)[:, None]
    picked = fine_flat[fine_index]
    diff = values - picked
    distances = jnp.mean(diff * diff, axis=1)
    return coarse_new, fine_flat.reshape(K, F, D), distances
```

```python
import functools

import jax
import jax.numpy as jnp
from jax import lax
from jax.experimental import pallas as pl
from jax.experimental.pallas import tpu as pltpu
from jax.sharding import PartitionSpec as P

MESH = pl.DeviceIdType.MESH
LANES = 128


def greet(owners, groups, own, grp, with_all):
    barrier = pltpu.get_barrier_semaphore()

    def one(k, carry):
        for j in range(groups):
            pl.semaphore_signal(
                barrier,
                inc=1,
                device_id=(lax.rem(own + k, owners), lax.rem(grp + j, groups)),
                device_id_type=MESH,
            )
        return carry

    lax.fori_loop(1, owners, one, 0)
    for j in range(1, groups):
        pl.semaphore_signal(
            barrier, inc=1, device_id=(own, lax.rem(grp + j, groups)), device_id_type=MESH
        )
    pl.semaphore_wait(barrier, owners * groups - 1)


def send_kernel(owners, groups, slots, emb, pos, index, got, got_index, packed, send_sem, recv_sem, isend, irecv, own_sem):
    own, grp = lax.axis_index("rows"), lax.axis_index("grp")
    me = own * groups + grp
    block = groups * slots
    mine = pl.ds(pl.multiple_of(me * slots, slots), slots)
    greet(owners, groups, own, grp, True)

    def pack(owner):
        at = pl.multiple_of(owner * block, block)
        slot = lax.broadcasted_iota(jnp.int32, (block, emb.shape[0]), 0) + at
        hit = jnp.where(slot == pos[...], 1.0, 0.0).astype(jnp.bfloat16)
        packed[pl.ds(at, block), :] = jnp.dot(
            hit, emb[...], preferred_element_type=jnp.float32
        ).astype(jnp.bfloat16)

    def copies(k, j):
        owner, group = lax.rem(own + k, owners), lax.rem(grp + j, groups)
        dest = owner * groups + group
        at = k * groups + j
        rows = pltpu.make_async_remote_copy(
            src_ref=packed.at[pl.ds(pl.multiple_of(dest * slots, slots), slots)],
            dst_ref=got.at[mine],
            send_sem=send_sem.at[at],
            recv_sem=recv_sem.at[at],
            device_id=(owner, group),
            device_id_type=MESH,
        )
        ids = pltpu.make_async_remote_copy(
            src_ref=index.at[dest],
            dst_ref=got_index.at[me],
            send_sem=isend.at[at],
            recv_sem=irecv.at[at],
            device_id=(owner, group),
            device_id_type=MESH,
        )
        return rows, ids

    def step(k, carry):
        pack(lax.rem(own + k, owners))
        for j in range(groups):
            rows, ids = copies(k, j)
            rows.start()
            ids.start()
        return carry

    lax.fori_loop(1, owners, step, 0)
    pack(own)
    for j in range(1, groups):
        rows, ids = copies(0, j)
        rows.start()
        ids.start()
    here = pltpu.make_async_copy(packed.at[mine], got.at[mine], own_sem.at[0])
    here_ids = pltpu.make_async_copy(index.at[me], got_index.at[me], own_sem.at[1])
    here.start()
    here_ids.start()
    here.wait()
    here_ids.wait()
    for j in range(1, groups):
        rows, ids = copies(0, j)
        rows.wait()
        ids.wait()

    def finish(k, carry):
        for j in range(groups):
            rows, ids = copies(k, j)
            rows.wait()
            ids.wait()
        return carry

    lax.fori_loop(1, owners, finish, 0)


def update_kernel(chunk, per_group, idx_s, idx_col, idx_row, rows, old, new, dist, coarse, held, work, in_sem, out_sem):
    count, width = old.shape
    total = rows.shape[0]
    per_owner = coarse.shape[0]
    load = pltpu.make_async_copy(old, held.at[pl.ds(0, count)], in_sem)
    load.start()
    held[count:, :] = jnp.zeros((held.shape[0] - count, width), jnp.float32)
    owner_of = lax.broadcasted_iota(jnp.int32, (per_owner, total), 0)
    low = owner_of * per_group
    ids = idx_row[...]
    part = jnp.where((ids >= low) & (ids < low + per_group) & (ids < count), 1.0, 0.0)
    coarse[:, :width] = jnp.dot(
        part.astype(jnp.bfloat16), rows[...], preferred_element_type=jnp.float32
    )
    coarse[:, width:] = jnp.broadcast_to(
        jnp.sum(part, axis=1, keepdims=True), (per_owner, LANES)
    )
    load.wait()

    def gather(i, carry):
        at = idx_s[i]
        work[pl.ds(i, 1), :] = held[pl.ds(at, 1), :]
        return carry

    lax.fori_loop(0, total, gather, 0, unroll=8)

    def combine(c, carry):
        at = pl.ds(pl.multiple_of(c * chunk, chunk), chunk)
        col = idx_col[at, :]
        same = jnp.where(col == ids, 1.0, 0.0)
        sums = jnp.dot(same.astype(jnp.bfloat16), rows[...], preferred_element_type=jnp.float32)
        number = jnp.sum(same, axis=1, keepdims=True)
        fresh = (work[at, :] + sums) / (1.0 + number)
        diff = rows[at, :].astype(jnp.float32) - fresh
        dist[at, :] = jnp.broadcast_to(
            jnp.sum(diff * diff, axis=1, keepdims=True) / width, (chunk, LANES)
        )
        work[at, :] = fresh
        return carry

    lax.fori_loop(0, total // chunk, combine, 0)

    def scatter(i, carry):
        at = idx_s[i]
        held[pl.ds(at, 1), :] = work[pl.ds(i, 1), :]
        return carry

    lax.fori_loop(0, total, scatter, 0, unroll=8)
    save = pltpu.make_async_copy(held.at[pl.ds(0, count)], new, out_sem)
    save.start()
    save.wait()


def return_kernel(owners, groups, dist, coarse, got_dist, got_coarse, dsend, drecv, csend, crecv, own_sem):
    own, grp = lax.axis_index("rows"), lax.axis_index("grp")
    me = own * groups + grp
    share = coarse.shape[0] // groups
    greet(owners, groups, own, grp, True)

    def sums(j):
        group = lax.rem(grp + j, groups)
        return pltpu.make_async_remote_copy(
            src_ref=coarse.at[pl.ds(pl.multiple_of(group * share, share), share)],
            dst_ref=got_coarse.at[grp],
            send_sem=csend.at[j],
            recv_sem=crecv.at[j],
            device_id=(own, group),
            device_id_type=MESH,
        )

    def back(k, j):
        owner, group = lax.rem(own + k, owners), lax.rem(grp + j, groups)
        return pltpu.make_async_remote_copy(
            src_ref=dist.at[owner * groups + group],
            dst_ref=got_dist.at[me],
            send_sem=dsend.at[k * groups + j],
            recv_sem=drecv.at[k * groups + j],
            device_id=(owner, group),
            device_id_type=MESH,
        )

    for j in range(1, groups):
        sums(j).start()

    def step(k, carry):
        for j in range(groups):
            back(k, j).start()
        return carry

    lax.fori_loop(1, owners, step, 0)
    for j in range(1, groups):
        back(0, j).start()
    here = pltpu.make_async_copy(dist.at[me], got_dist.at[me], own_sem.at[0])
    here_sums = pltpu.make_async_copy(
        coarse.at[pl.ds(pl.multiple_of(grp * share, share), share)], got_coarse.at[grp], own_sem.at[1]
    )
    here.start()
    here_sums.start()
    here.wait()
    here_sums.wait()
    for j in range(1, groups):
        back(0, j).wait()
        sums(j).wait()

    def finish(k, carry):
        for j in range(groups):
            back(k, j).wait()
        return carry

    lax.fori_loop(1, owners, finish, 0)


def on_device(embeddings, coarse_ids, fine_ids, coarse_old, fine_old):
    owners = lax.axis_size("rows")
    groups = lax.axis_size("grp")
    dests = owners * groups
    local_rows, width = embeddings.shape
    slots = max(2, 2 * local_rows // dests)
    slots = (slots + 15) // 16 * 16
    total = dests * slots
    per_owner, per_group = fine_old.shape[:2]
    count = per_owner * per_group
    target = coarse_ids // per_owner * groups + fine_ids // per_group
    local_index = coarse_ids % per_owner * per_group + fine_ids % per_group
    before = jnp.arange(local_rows)[None, :] < jnp.arange(local_rows)[:, None]
    rank = jnp.sum(((target[:, None] == target[None, :]) & before).astype(jnp.int32), axis=1)
    position = target * slots + rank
    slot_ids = jnp.arange(total, dtype=jnp.int32)
    send_index = jnp.min(
        jnp.where(slot_ids[:, None] == position[None, :], local_index[None, :], count), axis=1
    )
    send_index = jnp.pad(send_index.reshape(dests, 1, slots), ((0, 0), (0, 0), (0, LANES - slots)))
    vmem = pl.BlockSpec(memory_space=pltpu.VMEM)
    hbm = pl.BlockSpec(memory_space=pl.ANY)
    sems = pltpu.SemaphoreType.DMA
    got, got_index = pl.pallas_call(
        functools.partial(send_kernel, owners, groups, slots),
        out_shape=(
            jax.ShapeDtypeStruct((total, width), jnp.bfloat16),
            jax.ShapeDtypeStruct((dests, 1, LANES), jnp.int32),
        ),
        in_specs=[vmem, vmem, vmem],
        out_specs=(hbm, vmem),
        scratch_shapes=[
            pltpu.VMEM((total, width), jnp.bfloat16),
            sems((dests,)),
            sems((dests,)),
            sems((dests,)),
            sems((dests,)),
            sems((2,)),
        ],
        compiler_params=pltpu.CompilerParams(
            collective_id=0, has_side_effects=True, vmem_limit_bytes=32 * 2**20
        ),
        name="send_rows",
    )(embeddings, position.reshape(1, local_rows), send_index)
    index = got_index[:, 0, :slots].reshape(total)
    chunk = min(total, 256)
    new, dist, coarse = pl.pallas_call(
        functools.partial(update_kernel, chunk, per_group),
        out_shape=(
            jax.ShapeDtypeStruct((count, width), jnp.float32),
            jax.ShapeDtypeStruct((total, LANES), jnp.float32),
            jax.ShapeDtypeStruct((per_owner, width + LANES), jnp.float32),
        ),
        in_specs=[pl.BlockSpec(memory_space=pltpu.SMEM), vmem, vmem, vmem, hbm],
        out_specs=(hbm, vmem, vmem),
        scratch_shapes=[
            pltpu.VMEM((count + 8, width), jnp.float32),
            pltpu.VMEM((total, width), jnp.float32),
            sems,
            sems,
        ],
        compiler_params=pltpu.CompilerParams(vmem_limit_bytes=56 * 2**20),
        name="update",
    )(index, index.reshape(total, 1), index.reshape(1, total), got, fine_old.reshape(count, width))
    dist_back = jnp.pad(
        dist[:, 0].reshape(dests, 1, slots), ((0, 0), (0, 0), (0, LANES - slots))
    )
    got_dist, got_coarse = pl.pallas_call(
        functools.partial(return_kernel, owners, groups),
        out_shape=(
            jax.ShapeDtypeStruct((dests, 1, LANES), jnp.float32),
            jax.ShapeDtypeStruct((groups, per_owner // groups, width + LANES), jnp.float32),
        ),
        in_specs=[vmem, vmem],
        out_specs=(vmem, vmem),
        scratch_shapes=[
            sems((dests,)),
            sems((dests,)),
            sems((groups,)),
            sems((groups,)),
            sems((2,)),
        ],
        compiler_params=pltpu.CompilerParams(
            collective_id=1, has_side_effects=True, vmem_limit_bytes=32 * 2**20
        ),
        name="send_back",
    )(dist_back, coarse)
    returned = got_dist[:, 0, :slots].reshape(total)
    distances = jnp.sum(
        jnp.where(slot_ids[None, :] == position[:, None], returned[None, :], 0.0), axis=1
    )
    sums = jnp.sum(got_coarse, axis=0)
    coarse_new = (coarse_old + sums[:, :width]) / (1.0 + sums[:, width : width + 1])
    return coarse_new, new.reshape(fine_old.shape), distances


def solution(mesh):
    return jax.shard_map(
        on_device,
        mesh=mesh,
        in_specs=(
            P(("rows", "grp"), None),
            P(("rows", "grp")),
            P(("rows", "grp")),
            P(("rows", "grp"), None),
            P("rows", "grp", None),
        ),
        out_specs=(P(("rows", "grp"), None), P("rows", "grp", None), P(("rows", "grp"))),
        check_vma=False,
    )
```

```python
import functools

import jax
import jax.numpy as jnp
from jax import lax
from jax.experimental import pallas as pl
from jax.experimental.pallas import tpu as pltpu
from jax.sharding import PartitionSpec as P

MESH = pl.DeviceIdType.MESH
LANES = 128


def greet(owners, groups, own, grp):
    barrier = pltpu.get_barrier_semaphore()

    def one(k, carry):
        for j in range(groups):
            pl.semaphore_signal(
                barrier,
                inc=1,
                device_id=(lax.rem(own + k, owners), lax.rem(grp + j, groups)),
                device_id_type=MESH,
            )
        return carry

    lax.fori_loop(1, owners, one, 0)
    for j in range(1, groups):
        pl.semaphore_signal(
            barrier, inc=1, device_id=(own, lax.rem(grp + j, groups)), device_id_type=MESH
        )
    pl.semaphore_wait(barrier, owners * groups - 1)


def send_kernel(owners, groups, slots, emb_hbm, old, pos, index, got, got_index, held, packed, send_sem, recv_sem, isend, irecv, own_sem, emb):
    own, grp = lax.axis_index("rows"), lax.axis_index("grp")
    me = own * groups + grp
    block = groups * slots
    mine = pl.ds(pl.multiple_of(me * slots, slots), slots)
    fetch = pltpu.make_async_copy(emb_hbm, emb, own_sem.at[2])
    fetch.start()
    load = pltpu.make_async_copy(old, held, own_sem.at[3])
    load.start()
    greet(owners, groups, own, grp)
    fetch.wait()

    def pack(owner):
        at = pl.multiple_of(owner * block, block)
        slot = lax.broadcasted_iota(jnp.int32, (block, emb.shape[0]), 0) + at
        hit = jnp.where(slot == pos[...], 1.0, 0.0).astype(jnp.bfloat16)
        packed[pl.ds(at, block), :] = jnp.dot(
            hit, emb[...], preferred_element_type=jnp.float32
        ).astype(jnp.bfloat16)

    def copies(k, j):
        owner, group = lax.rem(own + k, owners), lax.rem(grp + j, groups)
        dest = owner * groups + group
        at = k * groups + j
        rows = pltpu.make_async_remote_copy(
            src_ref=packed.at[pl.ds(pl.multiple_of(dest * slots, slots), slots)],
            dst_ref=got.at[mine],
            send_sem=send_sem.at[at],
            recv_sem=recv_sem.at[at],
            device_id=(owner, group),
            device_id_type=MESH,
        )
        ids = pltpu.make_async_remote_copy(
            src_ref=index.at[dest],
            dst_ref=got_index.at[me],
            send_sem=isend.at[at],
            recv_sem=irecv.at[at],
            device_id=(owner, group),
            device_id_type=MESH,
        )
        return rows, ids

    def step(k, carry):
        pack(lax.rem(own + k, owners))
        for j in range(groups):
            rows, ids = copies(k, j)
            rows.start()
            ids.start()
        return carry

    lax.fori_loop(1, owners, step, 0)
    pack(own)
    for j in range(1, groups):
        rows, ids = copies(0, j)
        rows.start()
        ids.start()
    here = pltpu.make_async_copy(packed.at[mine], got.at[mine], own_sem.at[0])
    here_ids = pltpu.make_async_copy(index.at[me], got_index.at[me], own_sem.at[1])
    here.start()
    here_ids.start()
    here.wait()
    here_ids.wait()
    for j in range(1, groups):
        rows, ids = copies(0, j)
        rows.wait()
        ids.wait()

    def finish(k, carry):
        for j in range(groups):
            rows, ids = copies(k, j)
            rows.wait()
            ids.wait()
        return carry

    lax.fori_loop(1, owners, finish, 0)
    load.wait()


def coarse_kernel(slots, groups, per_group, count, index, rows, held, ids_row, ids_col, kept, *parts):
    dests, total = index.shape[0], rows.shape[0]
    share, width = parts[0].shape[0], rows.shape[1]
    ids = jnp.concatenate([index[s][:, :slots] for s in range(dests)], axis=1)
    ids_row[...] = ids
    ids_col[...] = jnp.transpose(jnp.broadcast_to(ids, (LANES, total)))
    grp = lax.axis_index("grp")
    for j, part in enumerate(parts):
        first = lax.rem(grp + j, groups) * share
        low = (lax.broadcasted_iota(jnp.int32, (share, total), 0) + first) * per_group
        hit = jnp.where((ids >= low) & (ids < low + per_group) & (ids < count), 1.0, 0.0)
        part[:, :width] = jnp.dot(
            hit.astype(jnp.bfloat16), rows[...], preferred_element_type=jnp.float32
        )
        part[:, width:] = jnp.broadcast_to(jnp.sum(hit, axis=1, keepdims=True), (share, LANES))


def update_kernel(chunk, slots, index, ids_col, ids_row, rows, held, new, dist, updated, work, out_sem):
    count, width = held.shape
    total = rows.shape[0]
    dests = index.shape[0]
    step = 8
    ids = ids_row[...]

    def each_row(act):
        def source(s, carry):
            def some(i, carry):
                for u in range(step):
                    slot = jnp.minimum(i * step + u, index[s, 0, slots] - 1)
                    act(index[s, 0, slot], s * slots + slot)
                return carry

            return lax.fori_loop(0, (index[s, 0, slots] + step - 1) // step, some, carry)

        lax.fori_loop(0, dests, source, 0)

    def gather(at, row):
        work[pl.ds(row, 1), :] = updated[pl.ds(at, 1), :]

    def scatter(at, row):
        updated[pl.ds(at, 1), :] = work[pl.ds(row, 1), :]

    each_row(gather)

    def combine(c, carry):
        at = pl.ds(pl.multiple_of(c * chunk, chunk), chunk)
        same = jnp.where(ids_col[at, :1] == ids, 1.0, 0.0)
        sums = jnp.dot(same.astype(jnp.bfloat16), rows[...], preferred_element_type=jnp.float32)
        fresh = (work[at, :] + sums) / (1.0 + jnp.sum(same, axis=1, keepdims=True))
        diff = rows[at, :].astype(jnp.float32) - fresh
        work[at, :] = fresh
        far = jnp.broadcast_to(jnp.sum(diff * diff, axis=1, keepdims=True) / width, (chunk, LANES))
        line = jnp.transpose(far)[:1, :]
        for p in range(chunk // slots):
            dist[c * (chunk // slots) + p] = jnp.concatenate(
                [line[:, p * slots : (p + 1) * slots], jnp.zeros((1, LANES - slots), jnp.float32)], axis=1
            )
        return carry

    lax.fori_loop(0, total // chunk, combine, 0)
    each_row(scatter)
    save = pltpu.make_async_copy(updated, new, out_sem)
    save.start()
    save.wait()


def return_kernel(owners, groups, dist, got_dist, dsend, drecv, own_sem):
    own, grp = lax.axis_index("rows"), lax.axis_index("grp")
    me = own * groups + grp
    greet(owners, groups, own, grp)

    def back(k, j):
        owner, group = lax.rem(own + k, owners), lax.rem(grp + j, groups)
        return pltpu.make_async_remote_copy(
            src_ref=dist.at[owner * groups + group],
            dst_ref=got_dist.at[me],
            send_sem=dsend.at[k * groups + j],
            recv_sem=drecv.at[k * groups + j],
            device_id=(owner, group),
            device_id_type=MESH,
        )

    def step(k, carry):
        for j in range(groups):
            back(k, j).start()
        return carry

    lax.fori_loop(1, owners, step, 0)
    for j in range(1, groups):
        back(0, j).start()
    here = pltpu.make_async_copy(dist.at[me], got_dist.at[me], own_sem)
    here.start()
    here.wait()
    for j in range(1, groups):
        back(0, j).wait()

    def finish(k, carry):
        for j in range(groups):
            back(k, j).wait()
        return carry

    lax.fori_loop(1, owners, finish, 0)


def on_device(embeddings, coarse_ids, fine_ids, coarse_old, fine_old):
    owners = lax.axis_size("rows")
    groups = lax.axis_size("grp")
    dests = owners * groups
    local_rows, width = embeddings.shape
    slots = max(2, 2 * local_rows // dests)
    slots = (slots + 15) // 16 * 16
    total = dests * slots
    per_owner, per_group = fine_old.shape[:2]
    count = per_owner * per_group
    target = coarse_ids // per_owner * groups + fine_ids // per_group
    local_index = coarse_ids % per_owner * per_group + fine_ids % per_group
    before = jnp.arange(local_rows)[None, :] < jnp.arange(local_rows)[:, None]
    rank = jnp.sum(((target[:, None] == target[None, :]) & before).astype(jnp.int32), axis=1)
    position = target * slots + rank
    slot_ids = jnp.arange(total, dtype=jnp.int32)
    send_index = jnp.min(
        jnp.where(slot_ids[:, None] == position[None, :], local_index[None, :], count), axis=1
    )
    filled = jnp.sum((target[None, :] == jnp.arange(dests)[:, None]).astype(jnp.int32), axis=1)
    send_index = jnp.concatenate(
        [
            send_index.reshape(dests, 1, slots),
            jnp.broadcast_to(filled[:, None, None], (dests, 1, LANES - slots)),
        ],
        axis=2,
    )
    spare = 8 * 2**20
    vmem = pl.BlockSpec(memory_space=pltpu.VMEM)
    hbm = pl.BlockSpec(memory_space=pl.ANY)
    sems = pltpu.SemaphoreType.DMA
    got, got_index, held = pl.pallas_call(
        functools.partial(send_kernel, owners, groups, slots),
        out_shape=(
            jax.ShapeDtypeStruct((total, width), jnp.bfloat16),
            jax.ShapeDtypeStruct((dests, 1, LANES), jnp.int32),
            jax.ShapeDtypeStruct((count, width), jnp.float32),
        ),
        in_specs=[hbm, hbm, vmem, vmem],
        out_specs=(vmem, vmem, vmem),
        scratch_shapes=[
            pltpu.VMEM((total, width), jnp.bfloat16),
            sems((dests,)),
            sems((dests,)),
            sems((dests,)),
            sems((dests,)),
            sems((4,)),
            pltpu.VMEM((local_rows, width), jnp.bfloat16),
        ],
        compiler_params=pltpu.CompilerParams(
            collective_id=0,
            has_side_effects=True,
            vmem_limit_bytes=total * width * 4 + local_rows * width * 2 + count * width * 4 + spare,
        ),
        cost_estimate=pl.CostEstimate(
            flops=2 * total * local_rows * width,
            bytes_accessed=64 * total * width,
            transcendentals=0,
            remote_bytes_transferred=2 * total * width,
        ),
        name="send_rows",
    )(embeddings, fine_old.reshape(count, width), position.reshape(1, local_rows), send_index)
    share = per_owner // groups
    ids_row, ids_col, held, *parts = pl.pallas_call(
        functools.partial(coarse_kernel, slots, groups, per_group, count),
        out_shape=[
            jax.ShapeDtypeStruct((1, total), jnp.int32),
            jax.ShapeDtypeStruct((total, LANES), jnp.int32),
            jax.ShapeDtypeStruct((count, width), jnp.float32),
        ]
        + [jax.ShapeDtypeStruct((share, width + LANES), jnp.float32)] * groups,
        in_specs=[vmem, vmem, vmem],
        out_specs=[vmem] * (3 + groups),
        input_output_aliases={2: 2},
        compiler_params=pltpu.CompilerParams(
            vmem_limit_bytes=total * width * 2 + per_owner * total * 12 + per_owner * width * 4 + spare
        ),
        name="coarse_part",
    )(got_index, got, held)
    sums = parts[0]
    for j in range(1, groups):
        around = [(g, (g + j) % groups) for g in range(groups)]
        sums = sums + lax.ppermute(parts[j], "grp", around)
    chunk = min(total, 256)
    new, dist, _ = pl.pallas_call(
        functools.partial(update_kernel, chunk, slots),
        out_shape=(
            jax.ShapeDtypeStruct((count, width), jnp.float32),
            jax.ShapeDtypeStruct((dests, 1, LANES), jnp.float32),
            jax.ShapeDtypeStruct((count, width), jnp.float32),
        ),
        in_specs=[pl.BlockSpec(memory_space=pltpu.SMEM), vmem, vmem, vmem, vmem],
        out_specs=(hbm, vmem, vmem),
        input_output_aliases={4: 2},
        scratch_shapes=[
            pltpu.VMEM((total, width), jnp.float32),
            sems,
        ],
        compiler_params=pltpu.CompilerParams(
            vmem_limit_bytes=total * width * 6 + spare
        ),
        cost_estimate=pl.CostEstimate(
            flops=2 * total * total * width, bytes_accessed=8 * count * width, transcendentals=0
        ),
        name="update",
    )(got_index, ids_col, ids_row, got, held)
    got_dist = pl.pallas_call(
        functools.partial(return_kernel, owners, groups),
        out_shape=jax.ShapeDtypeStruct((dests, 1, LANES), jnp.float32),
        in_specs=[vmem],
        out_specs=vmem,
        scratch_shapes=[sems((dests,)), sems((dests,)), sems],
        compiler_params=pltpu.CompilerParams(collective_id=1, has_side_effects=True),
        name="send_back",
    )(dist)
    returned = got_dist[:, 0, :slots].reshape(total)
    distances = jnp.sum(
        jnp.where(slot_ids[None, :] == position[:, None], returned[None, :], 0.0), axis=1
    )
    coarse_new = (coarse_old + sums[:, :width]) / (1.0 + sums[:, width : width + 1])
    return coarse_new, new.reshape(fine_old.shape), distances


def solution(mesh):
    return jax.shard_map(
        on_device,
        mesh=mesh,
        in_specs=(
            P(("rows", "grp"), None),
            P(("rows", "grp")),
            P(("rows", "grp")),
            P(("rows", "grp"), None),
            P("rows", "grp", None),
        ),
        out_specs=(P(("rows", "grp"), None), P("rows", "grp", None), P(("rows", "grp"))),
        check_vma=False,
    )
```

```python
import functools

import jax
import jax.numpy as jnp
from jax import lax
from jax.experimental import pallas as pl
from jax.experimental.pallas import tpu as pltpu
from jax.sharding import PartitionSpec as P

MESH = pl.DeviceIdType.MESH
LANES = 128


def greet(owners, groups, own, grp):
    barrier = pltpu.get_barrier_semaphore()

    def one(k, carry):
        for j in range(groups):
            pl.semaphore_signal(
                barrier,
                inc=1,
                device_id=(lax.rem(own + k, owners), lax.rem(grp + j, groups)),
                device_id_type=MESH,
            )
        return carry

    lax.fori_loop(1, owners, one, 0)
    for j in range(1, groups):
        pl.semaphore_signal(
            barrier, inc=1, device_id=(own, lax.rem(grp + j, groups)), device_id_type=MESH
        )
    pl.semaphore_wait(barrier, owners * groups - 1)


def send_kernel(owners, groups, slots, emb_hbm, old, pos, index, got, got_index, held, packed, send_sem, recv_sem, isend, irecv, own_sem, emb):
    own, grp = lax.axis_index("rows"), lax.axis_index("grp")
    me = own * groups + grp
    block = groups * slots
    mine = pl.ds(pl.multiple_of(me * slots, slots), slots)
    fetch = pltpu.make_async_copy(emb_hbm, emb, own_sem.at[2])
    fetch.start()
    load = pltpu.make_async_copy(old, held, own_sem.at[3])
    load.start()
    greet(owners, groups, own, grp)
    fetch.wait()

    halves = 2 if owners % 2 == 0 else 1
    half = owners // halves

    def partner(k):
        cross = (k + 1) % halves
        i = lax.rem(own % half + k // halves + 1 - cross, half)
        return lax.rem(own // half + cross, halves) * half + i

    def pack(owner):
        at = pl.multiple_of(owner * block, block)
        slot = lax.broadcasted_iota(jnp.int32, (block, emb.shape[0]), 0) + at
        hit = jnp.where(slot == pos[...], 1.0, 0.0).astype(jnp.bfloat16)
        packed[pl.ds(at, block), :] = jnp.dot(
            hit, emb[...], preferred_element_type=jnp.float32
        ).astype(jnp.bfloat16)

    def copies(k, j):
        owner, group = partner(k), lax.rem(grp + j, groups)
        dest = owner * groups + group
        at = k * groups + j
        rows = pltpu.make_async_remote_copy(
            src_ref=packed.at[pl.ds(pl.multiple_of(dest * slots, slots), slots)],
            dst_ref=got.at[mine],
            send_sem=send_sem.at[at],
            recv_sem=recv_sem.at[at],
            device_id=(owner, group),
            device_id_type=MESH,
        )
        ids = pltpu.make_async_remote_copy(
            src_ref=index.at[dest],
            dst_ref=got_index.at[me],
            send_sem=isend.at[at],
            recv_sem=irecv.at[at],
            device_id=(owner, group),
            device_id_type=MESH,
        )
        return rows, ids

    def step(k, carry):
        pack(partner(k))
        for j in range(groups):
            rows, ids = copies(k, j)
            rows.start()
            ids.start()
        return carry

    lax.fori_loop(0, owners - 1, step, 0)
    pack(own)
    for j in range(1, groups):
        rows, ids = copies(owners - 1, j)
        rows.start()
        ids.start()
    here = pltpu.make_async_copy(packed.at[mine], got.at[mine], own_sem.at[0])
    here_ids = pltpu.make_async_copy(index.at[me], got_index.at[me], own_sem.at[1])
    here.start()
    here_ids.start()
    here.wait()
    here_ids.wait()
    for j in range(1, groups):
        rows, ids = copies(owners - 1, j)
        rows.wait()
        ids.wait()

    def finish(k, carry):
        for j in range(groups):
            rows, ids = copies(k, j)
            rows.wait()
            ids.wait()
        return carry

    lax.fori_loop(0, owners - 1, finish, 0)
    load.wait()


def coarse_kernel(slots, groups, per_group, count, index, rows, held, ids_row, ids_col, kept, *parts):
    dests, total = index.shape[0], rows.shape[0]
    share, width = parts[0].shape[0], rows.shape[1]
    ids = jnp.concatenate([index[s][:, :slots] for s in range(dests)], axis=1)
    ids_row[...] = ids
    ids_col[...] = jnp.transpose(jnp.broadcast_to(ids, (LANES, total)))
    grp = lax.axis_index("grp")
    for j, part in enumerate(parts):
        first = lax.rem(grp + j, groups) * share
        low = (lax.broadcasted_iota(jnp.int32, (share, total), 0) + first) * per_group
        hit = jnp.where((ids >= low) & (ids < low + per_group) & (ids < count), 1.0, 0.0)
        part[:, :width] = jnp.dot(
            hit.astype(jnp.bfloat16), rows[...], preferred_element_type=jnp.float32
        )
        part[:, width:] = jnp.broadcast_to(jnp.sum(hit, axis=1, keepdims=True), (share, LANES))


def update_kernel(chunk, slots, index, ids_col, ids_row, rows, held, new, dist, updated, work, out_sem):
    count, width = held.shape
    total = rows.shape[0]
    dests = index.shape[0]
    step = 8
    ids = ids_row[...]

    def each_row(act):
        def source(s, carry):
            def some(i, carry):
                for u in range(step):
                    slot = jnp.minimum(i * step + u, index[s, 0, slots] - 1)
                    act(index[s, 0, slot], s * slots + slot)
                return carry

            return lax.fori_loop(0, (index[s, 0, slots] + step - 1) // step, some, carry)

        lax.fori_loop(0, dests, source, 0)

    def gather(at, row):
        work[pl.ds(row, 1), :] = updated[pl.ds(at, 1), :]

    def scatter(at, row):
        updated[pl.ds(at, 1), :] = work[pl.ds(row, 1), :]

    each_row(gather)

    def combine(c, carry):
        at = pl.ds(pl.multiple_of(c * chunk, chunk), chunk)
        same = jnp.where(ids_col[at, :1] == ids, 1.0, 0.0)
        sums = jnp.dot(same.astype(jnp.bfloat16), rows[...], preferred_element_type=jnp.float32)
        fresh = (work[at, :] + sums) / (1.0 + jnp.sum(same, axis=1, keepdims=True))
        diff = rows[at, :].astype(jnp.float32) - fresh
        work[at, :] = fresh
        far = jnp.broadcast_to(jnp.sum(diff * diff, axis=1, keepdims=True) / width, (chunk, LANES))
        line = jnp.transpose(far)[:1, :]
        for p in range(chunk // slots):
            dist[c * (chunk // slots) + p] = jnp.concatenate(
                [line[:, p * slots : (p + 1) * slots], jnp.zeros((1, LANES - slots), jnp.float32)], axis=1
            )
        return carry

    lax.fori_loop(0, total // chunk, combine, 0)
    each_row(scatter)
    save = pltpu.make_async_copy(updated, new, out_sem)
    save.start()
    save.wait()


def return_kernel(owners, groups, dist, got_dist, dsend, drecv, own_sem):
    own, grp = lax.axis_index("rows"), lax.axis_index("grp")
    me = own * groups + grp
    greet(owners, groups, own, grp)

    def back(k, j):
        owner, group = lax.rem(own + k, owners), lax.rem(grp + j, groups)
        return pltpu.make_async_remote_copy(
            src_ref=dist.at[owner * groups + group],
            dst_ref=got_dist.at[me],
            send_sem=dsend.at[k * groups + j],
            recv_sem=drecv.at[k * groups + j],
            device_id=(owner, group),
            device_id_type=MESH,
        )

    def step(k, carry):
        for j in range(groups):
            back(k, j).start()
        return carry

    lax.fori_loop(1, owners, step, 0)
    for j in range(1, groups):
        back(0, j).start()
    here = pltpu.make_async_copy(dist.at[me], got_dist.at[me], own_sem)
    here.start()
    here.wait()
    for j in range(1, groups):
        back(0, j).wait()

    def finish(k, carry):
        for j in range(groups):
            back(k, j).wait()
        return carry

    lax.fori_loop(1, owners, finish, 0)


def on_device(embeddings, coarse_ids, fine_ids, coarse_old, fine_old):
    owners = lax.axis_size("rows")
    groups = lax.axis_size("grp")
    dests = owners * groups
    local_rows, width = embeddings.shape
    slots = max(2, 2 * local_rows // dests)
    slots = (slots + 15) // 16 * 16
    total = dests * slots
    per_owner, per_group = fine_old.shape[:2]
    count = per_owner * per_group
    target = coarse_ids // per_owner * groups + fine_ids // per_group
    local_index = coarse_ids % per_owner * per_group + fine_ids % per_group
    before = jnp.arange(local_rows)[None, :] < jnp.arange(local_rows)[:, None]
    rank = jnp.sum(((target[:, None] == target[None, :]) & before).astype(jnp.int32), axis=1)
    position = target * slots + rank
    slot_ids = jnp.arange(total, dtype=jnp.int32)
    send_index = jnp.min(
        jnp.where(slot_ids[:, None] == position[None, :], local_index[None, :], count), axis=1
    )
    filled = jnp.sum((target[None, :] == jnp.arange(dests)[:, None]).astype(jnp.int32), axis=1)
    send_index = jnp.concatenate(
        [
            send_index.reshape(dests, 1, slots),
            jnp.broadcast_to(filled[:, None, None], (dests, 1, LANES - slots)),
        ],
        axis=2,
    )
    spare = 8 * 2**20
    vmem = pl.BlockSpec(memory_space=pltpu.VMEM)
    hbm = pl.BlockSpec(memory_space=pl.ANY)
    sems = pltpu.SemaphoreType.DMA
    got, got_index, held = pl.pallas_call(
        functools.partial(send_kernel, owners, groups, slots),
        out_shape=(
            jax.ShapeDtypeStruct((total, width), jnp.bfloat16),
            jax.ShapeDtypeStruct((dests, 1, LANES), jnp.int32),
            jax.ShapeDtypeStruct((count, width), jnp.float32),
        ),
        in_specs=[pl.BlockSpec(memory_space=pltpu.HBM)] * 2 + [vmem, vmem],
        out_specs=(vmem, vmem, vmem),
        scratch_shapes=[
            pltpu.VMEM((total, width), jnp.bfloat16),
            sems((dests,)),
            sems((dests,)),
            sems((dests,)),
            sems((dests,)),
            sems((4,)),
            pltpu.VMEM((local_rows, width), jnp.bfloat16),
        ],
        compiler_params=pltpu.CompilerParams(
            collective_id=0,
            has_side_effects=True,
            vmem_limit_bytes=total * width * 4 + local_rows * width * 2 + count * width * 4 + spare,
        ),
        cost_estimate=pl.CostEstimate(
            flops=2 * total * local_rows * width,
            bytes_accessed=64 * total * width,
            transcendentals=0,
            remote_bytes_transferred=2 * total * width,
        ),
        name="send_rows",
    )(embeddings, fine_old.reshape(count, width), position.reshape(1, local_rows), send_index)
    share = per_owner // groups
    ids_row, ids_col, held, *parts = pl.pallas_call(
        functools.partial(coarse_kernel, slots, groups, per_group, count),
        out_shape=[
            jax.ShapeDtypeStruct((1, total), jnp.int32),
            jax.ShapeDtypeStruct((total, LANES), jnp.int32),
            jax.ShapeDtypeStruct((count, width), jnp.float32),
        ]
        + [jax.ShapeDtypeStruct((share, width + LANES), jnp.float32)] * groups,
        in_specs=[vmem, vmem, vmem],
        out_specs=[vmem] * (3 + groups),
        input_output_aliases={2: 2},
        compiler_params=pltpu.CompilerParams(
            vmem_limit_bytes=total * width * 2 + per_owner * total * 12 + per_owner * width * 4 + spare
        ),
        name="coarse_part",
    )(got_index, got, held)
    sums = parts[0]
    for j in range(1, groups):
        around = [(g, (g + j) % groups) for g in range(groups)]
        sums = sums + lax.ppermute(parts[j], "grp", around)
    chunk = min(total, 256)
    new, dist, _ = pl.pallas_call(
        functools.partial(update_kernel, chunk, slots),
        out_shape=(
            jax.ShapeDtypeStruct((count, width), jnp.float32),
            jax.ShapeDtypeStruct((dests, 1, LANES), jnp.float32),
            jax.ShapeDtypeStruct((count, width), jnp.float32),
        ),
        in_specs=[pl.BlockSpec(memory_space=pltpu.SMEM), vmem, vmem, vmem, vmem],
        out_specs=(hbm, vmem, vmem),
        input_output_aliases={4: 2},
        scratch_shapes=[
            pltpu.VMEM((total, width), jnp.float32),
            sems,
        ],
        compiler_params=pltpu.CompilerParams(
            vmem_limit_bytes=total * width * 6 + spare
        ),
        cost_estimate=pl.CostEstimate(
            flops=2 * total * total * width, bytes_accessed=8 * count * width, transcendentals=0
        ),
        name="update",
    )(got_index, ids_col, ids_row, got, held)
    got_dist = pl.pallas_call(
        functools.partial(return_kernel, owners, groups),
        out_shape=jax.ShapeDtypeStruct((dests, 1, LANES), jnp.float32),
        in_specs=[vmem],
        out_specs=vmem,
        scratch_shapes=[sems((dests,)), sems((dests,)), sems],
        compiler_params=pltpu.CompilerParams(
            collective_id=1, has_side_effects=True, vmem_limit_bytes=spare
        ),
        name="send_back",
    )(dist)
    returned = got_dist[:, 0, :slots].reshape(total)
    distances = jnp.sum(
        jnp.where(slot_ids[None, :] == position[:, None], returned[None, :], 0.0), axis=1
    )
    coarse_new = (coarse_old + sums[:, :width]) / (1.0 + sums[:, width : width + 1])
    return coarse_new, new.reshape(fine_old.shape), distances


def solution(mesh):
    return jax.shard_map(
        on_device,
        mesh=mesh,
        in_specs=(
            P(("rows", "grp"), None),
            P(("rows", "grp")),
            P(("rows", "grp")),
            P(("rows", "grp"), None),
            P("rows", "grp", None),
        ),
        out_specs=(P(("rows", "grp"), None), P("rows", "grp", None), P(("rows", "grp"))),
        check_vma=False,
    )
```

```python
import functools

import jax
import jax.numpy as jnp
from jax import lax
from jax.experimental import pallas as pl
from jax.experimental.pallas import tpu as pltpu
from jax.sharding import PartitionSpec as P

MESH = pl.DeviceIdType.MESH
LANES = 128


def greet(owners, groups, own, grp):
    barrier = pltpu.get_barrier_semaphore()

    def one(k, carry):
        for j in range(groups):
            pl.semaphore_signal(
                barrier,
                inc=1,
                device_id=(lax.rem(own + k, owners), lax.rem(grp + j, groups)),
                device_id_type=MESH,
            )
        return carry

    lax.fori_loop(1, owners, one, 0)
    for j in range(1, groups):
        pl.semaphore_signal(
            barrier, inc=1, device_id=(own, lax.rem(grp + j, groups)), device_id_type=MESH
        )
    pl.semaphore_wait(barrier, owners * groups - 1)


def send_kernel(owners, groups, slots, emb_hbm, old, pos, index, got, got_index, held, packed, send_sem, recv_sem, isend, irecv, own_sem, emb):
    own, grp = lax.axis_index("rows"), lax.axis_index("grp")
    me = own * groups + grp
    block = groups * slots
    mine = pl.ds(pl.multiple_of(me * slots, slots), slots)
    fetch = pltpu.make_async_copy(emb_hbm, emb, own_sem.at[2])
    fetch.start()
    load = pltpu.make_async_copy(old, held, own_sem.at[3])
    load.start()
    greet(owners, groups, own, grp)
    fetch.wait()

    halves = 2 if owners % 2 == 0 else 1
    half = owners // halves

    def partner(k):
        cross = (k + 1) % halves
        i = lax.rem(own % half + k // halves + 1 - cross, half)
        return lax.rem(own // half + cross, halves) * half + i

    def pack(owner):
        at = pl.multiple_of(owner * block, block)
        slot = lax.broadcasted_iota(jnp.int32, (block, emb.shape[0]), 0) + at
        hit = jnp.where(slot == pos[...], 1.0, 0.0).astype(jnp.bfloat16)
        packed[pl.ds(at, block), :] = jnp.dot(
            hit, emb[...], preferred_element_type=jnp.float32
        ).astype(jnp.bfloat16)

    def copies(k, j):
        owner, group = partner(k), lax.rem(grp + j, groups)
        dest = owner * groups + group
        at = k * groups + j
        rows = pltpu.make_async_remote_copy(
            src_ref=packed.at[pl.ds(pl.multiple_of(dest * slots, slots), slots)],
            dst_ref=got.at[mine],
            send_sem=send_sem.at[at],
            recv_sem=recv_sem.at[at],
            device_id=(owner, group),
            device_id_type=MESH,
        )
        ids = pltpu.make_async_remote_copy(
            src_ref=index.at[dest],
            dst_ref=got_index.at[me],
            send_sem=isend.at[at],
            recv_sem=irecv.at[at],
            device_id=(owner, group),
            device_id_type=MESH,
        )
        return rows, ids

    def step(k, carry):
        pack(partner(k))
        for j in range(groups):
            rows, ids = copies(k, j)
            rows.start()
            ids.start()
        return carry

    lax.fori_loop(0, owners - 1, step, 0)
    pack(own)
    for j in range(1, groups):
        rows, ids = copies(owners - 1, j)
        rows.start()
        ids.start()
    here = pltpu.make_async_copy(packed.at[mine], got.at[mine], own_sem.at[0])
    here_ids = pltpu.make_async_copy(index.at[me], got_index.at[me], own_sem.at[1])
    here.start()
    here_ids.start()
    here.wait()
    here_ids.wait()
    for j in range(1, groups):
        rows, ids = copies(owners - 1, j)
        rows.wait()
        ids.wait()

    def finish(k, carry):
        for j in range(groups):
            rows, ids = copies(k, j)
            rows.wait()
            ids.wait()
        return carry

    lax.fori_loop(0, owners - 1, finish, 0)
    load.wait()


def coarse_kernel(slots, groups, per_group, count, index, rows, held, ids_row, ids_col, kept, *parts):
    dests, total = index.shape[0], rows.shape[0]
    share, width = parts[0].shape[0], rows.shape[1]
    ids = jnp.concatenate([index[s][:, :slots] for s in range(dests)], axis=1)
    ids_row[...] = ids
    ids_col[...] = jnp.transpose(jnp.broadcast_to(ids, (LANES, total)))
    grp = lax.axis_index("grp")
    for j, part in enumerate(parts):
        first = lax.rem(grp + j, groups) * share
        low = (lax.broadcasted_iota(jnp.int32, (share, total), 0) + first) * per_group
        hit = jnp.where((ids >= low) & (ids < low + per_group) & (ids < count), 1.0, 0.0)
        part[:, :width] = jnp.dot(
            hit.astype(jnp.bfloat16), rows[...], preferred_element_type=jnp.float32
        )
        part[:, width:] = jnp.broadcast_to(jnp.sum(hit, axis=1, keepdims=True), (share, LANES))


def update_kernel(chunk, slots, index, ids_col, ids_row, rows, held, new, dist, updated, work, out_sem):
    count, width = held.shape
    total = rows.shape[0]
    dests = index.shape[0]
    step = 8
    ids = ids_row[...]

    def each_row(act):
        def source(s, carry):
            def some(i, carry):
                for u in range(step):
                    slot = jnp.minimum(i * step + u, index[s, 0, slots] - 1)
                    act(index[s, 0, slot], s * slots + slot)
                return carry

            return lax.fori_loop(0, (index[s, 0, slots] + step - 1) // step, some, carry)

        lax.fori_loop(0, dests, source, 0)

    def gather(at, row):
        work[pl.ds(row, 1), :] = updated[pl.ds(at, 1), :]

    each_row(gather)

    def combine(c, carry):
        at = pl.ds(pl.multiple_of(c * chunk, chunk), chunk)
        same = jnp.where(ids_col[at, :1] == ids, 1.0, 0.0)
        sums = jnp.dot(same.astype(jnp.bfloat16), rows[...], preferred_element_type=jnp.float32)
        part = 1.0 / (1.0 + jnp.sum(same, axis=1, keepdims=True))
        fresh = (work[at, :] + sums) * part
        diff = rows[at, :].astype(jnp.float32) - fresh
        work[at, :] = fresh
        far = jnp.broadcast_to(jnp.sum(diff * diff, axis=1, keepdims=True) / width, (chunk, LANES))
        line = jnp.transpose(far)[:1, :]
        for p in range(chunk // slots):
            dist[c * (chunk // slots) + p] = jnp.concatenate(
                [line[:, p * slots : (p + 1) * slots], jnp.zeros((1, LANES - slots), jnp.float32)], axis=1
            )
        return carry

    lax.fori_loop(0, total // chunk, combine, 0)
    saves = []
    for p in range(2):
        side = pl.ds(p * (width // 2), width // 2)

        def scatter(at, row):
            updated[pl.ds(at, 1), side] = work[pl.ds(row, 1), side]

        each_row(scatter)
        saves.append(pltpu.make_async_copy(updated.at[:, side], new.at[:, side], out_sem.at[p]))
        saves[p].start()
    for save in saves:
        save.wait()


def return_kernel(owners, groups, dist, got_dist, dsend, drecv, own_sem):
    own, grp = lax.axis_index("rows"), lax.axis_index("grp")
    me = own * groups + grp
    greet(owners, groups, own, grp)

    def back(k, j):
        owner, group = lax.rem(own + k, owners), lax.rem(grp + j, groups)
        return pltpu.make_async_remote_copy(
            src_ref=dist.at[owner * groups + group],
            dst_ref=got_dist.at[me],
            send_sem=dsend.at[k * groups + j],
            recv_sem=drecv.at[k * groups + j],
            device_id=(owner, group),
            device_id_type=MESH,
        )

    def step(k, carry):
        for j in range(groups):
            back(k, j).start()
        return carry

    lax.fori_loop(1, owners, step, 0)
    for j in range(1, groups):
        back(0, j).start()
    here = pltpu.make_async_copy(dist.at[me], got_dist.at[me], own_sem)
    here.start()
    here.wait()
    for j in range(1, groups):
        back(0, j).wait()

    def finish(k, carry):
        for j in range(groups):
            back(k, j).wait()
        return carry

    lax.fori_loop(1, owners, finish, 0)


def on_device(embeddings, coarse_ids, fine_ids, coarse_old, fine_old):
    owners = lax.axis_size("rows")
    groups = lax.axis_size("grp")
    dests = owners * groups
    local_rows, width = embeddings.shape
    slots = max(2, 2 * local_rows // dests)
    slots = (slots + 15) // 16 * 16
    total = dests * slots
    per_owner, per_group = fine_old.shape[:2]
    count = per_owner * per_group
    target = coarse_ids // per_owner * groups + fine_ids // per_group
    local_index = coarse_ids % per_owner * per_group + fine_ids % per_group
    before = jnp.arange(local_rows)[None, :] < jnp.arange(local_rows)[:, None]
    rank = jnp.sum(((target[:, None] == target[None, :]) & before).astype(jnp.int32), axis=1)
    position = target * slots + rank
    slot_ids = jnp.arange(total, dtype=jnp.int32)
    send_index = jnp.min(
        jnp.where(slot_ids[:, None] == position[None, :], local_index[None, :], count), axis=1
    )
    filled = jnp.sum((target[None, :] == jnp.arange(dests)[:, None]).astype(jnp.int32), axis=1)
    send_index = jnp.concatenate(
        [
            send_index.reshape(dests, 1, slots),
            jnp.broadcast_to(filled[:, None, None], (dests, 1, LANES - slots)),
        ],
        axis=2,
    )
    spare = 8 * 2**20
    vmem = pl.BlockSpec(memory_space=pltpu.VMEM)
    hbm = pl.BlockSpec(memory_space=pl.ANY)
    sems = pltpu.SemaphoreType.DMA
    got, got_index, held = pl.pallas_call(
        functools.partial(send_kernel, owners, groups, slots),
        out_shape=(
            jax.ShapeDtypeStruct((total, width), jnp.bfloat16),
            jax.ShapeDtypeStruct((dests, 1, LANES), jnp.int32),
            jax.ShapeDtypeStruct((count, width), jnp.float32),
        ),
        in_specs=[pl.BlockSpec(memory_space=pltpu.HBM)] * 2 + [vmem, vmem],
        out_specs=(vmem, vmem, vmem),
        scratch_shapes=[
            pltpu.VMEM((total, width), jnp.bfloat16),
            sems((dests,)),
            sems((dests,)),
            sems((dests,)),
            sems((dests,)),
            sems((4,)),
            pltpu.VMEM((local_rows, width), jnp.bfloat16),
        ],
        compiler_params=pltpu.CompilerParams(
            collective_id=0,
            has_side_effects=True,
            vmem_limit_bytes=total * width * 4 + local_rows * width * 2 + count * width * 4 + spare,
        ),
        cost_estimate=pl.CostEstimate(
            flops=2 * total * local_rows * width,
            bytes_accessed=64 * total * width,
            transcendentals=0,
            remote_bytes_transferred=2 * total * width,
        ),
        name="send_rows",
    )(embeddings, fine_old.reshape(count, width), position.reshape(1, local_rows), send_index)
    share = per_owner // groups
    ids_row, ids_col, held, *parts = pl.pallas_call(
        functools.partial(coarse_kernel, slots, groups, per_group, count),
        out_shape=[
            jax.ShapeDtypeStruct((1, total), jnp.int32),
            jax.ShapeDtypeStruct((total, LANES), jnp.int32),
            jax.ShapeDtypeStruct((count, width), jnp.float32),
        ]
        + [jax.ShapeDtypeStruct((share, width + LANES), jnp.float32)] * groups,
        in_specs=[vmem, vmem, vmem],
        out_specs=[vmem] * (3 + groups),
        input_output_aliases={2: 2},
        compiler_params=pltpu.CompilerParams(
            vmem_limit_bytes=total * width * 2 + per_owner * total * 12 + per_owner * width * 4 + spare
        ),
        name="coarse_part",
    )(got_index, got, held)
    sums = parts[0]
    for j in range(1, groups):
        around = [(g, (g + j) % groups) for g in range(groups)]
        sums = sums + lax.ppermute(parts[j], "grp", around)
    chunk = min(total, 256)
    new, dist, _ = pl.pallas_call(
        functools.partial(update_kernel, chunk, slots),
        out_shape=(
            jax.ShapeDtypeStruct((count, width), jnp.float32),
            jax.ShapeDtypeStruct((dests, 1, LANES), jnp.float32),
            jax.ShapeDtypeStruct((count, width), jnp.float32),
        ),
        in_specs=[pl.BlockSpec(memory_space=pltpu.SMEM), vmem, vmem, vmem, vmem],
        out_specs=(hbm, vmem, vmem),
        input_output_aliases={4: 2},
        scratch_shapes=[
            pltpu.VMEM((total, width), jnp.float32),
            sems((2,)),
        ],
        compiler_params=pltpu.CompilerParams(
            vmem_limit_bytes=total * width * 6 + spare
        ),
        cost_estimate=pl.CostEstimate(
            flops=2 * total * total * width, bytes_accessed=8 * count * width, transcendentals=0
        ),
        name="update",
    )(got_index, ids_col, ids_row, got, held)
    got_dist = pl.pallas_call(
        functools.partial(return_kernel, owners, groups),
        out_shape=jax.ShapeDtypeStruct((dests, 1, LANES), jnp.float32),
        in_specs=[vmem],
        out_specs=vmem,
        scratch_shapes=[sems((dests,)), sems((dests,)), sems],
        compiler_params=pltpu.CompilerParams(
            collective_id=1, has_side_effects=True, vmem_limit_bytes=spare
        ),
        name="send_back",
    )(dist)
    returned = got_dist[:, 0, :slots].reshape(total)
    distances = jnp.sum(
        jnp.where(slot_ids[None, :] == position[:, None], returned[None, :], 0.0), axis=1
    )
    coarse_new = (coarse_old + sums[:, :width]) / (1.0 + sums[:, width : width + 1])
    return coarse_new, new.reshape(fine_old.shape), distances


def solution(mesh):
    return jax.shard_map(
        on_device,
        mesh=mesh,
        in_specs=(
            P(("rows", "grp"), None),
            P(("rows", "grp")),
            P(("rows", "grp")),
            P(("rows", "grp"), None),
            P("rows", "grp", None),
        ),
        out_specs=(P(("rows", "grp"), None), P("rows", "grp", None), P(("rows", "grp"))),
        check_vma=False,
    )
```
